32 devices in a mesh: req: 4 (over y, x), exp: 8 (over z, core).
Axes of the slice: x: 2, y: 2, z: 4, core: 2. Of those that a mesh axis runs over, the one named last changes fastest.
Arguments:
- tokens: bfloat16 [8192, 1536], P(('req', 'exp')), may hold values from -6 to 6
- token_request_slot: int32 [32, 256], P(('req', 'exp')), may hold values from 0 to 3, never falling along the last dimension, each value on 1 to 128 neighbouring positions
- request_prompt: int32 [128], P(('req', 'exp')), may hold values from 0 to 7
- request_adapter: int32 [128], P(('req', 'exp')), may hold values from 0 to 15
- prompt_page_table: int32 [128], replicated, may hold values from 0 to 127, each once
- shared_prompt_cache: bfloat16 [128, 16, 512], P(('req', 'exp')), may hold values from -180 to 180
- routes: int32 [8192, 4], P(('req', 'exp')), may hold values from 0 to 7, all different within a row; in each aligned block of 256 rows (0 to 255, 256 to 511, ...) at most 192 rows name the same one
- attention_norm_gain: bfloat16 [1536], replicated, may hold values from 0.099609375 to 1.8984375
- query_matrix: bfloat16 [1536, 1536], replicated, may hold values from -0.15625 to 0.15625
- key_value_weight: bfloat16 [1536, 512], replicated, may hold values from -0.15625 to 0.15625
- attention_output_weight: bfloat16 [1536, 1536], replicated, may hold values from -0.15625 to 0.15625
- adapter_query_down: bfloat16 [1536, 256], replicated, may hold values from -0.15625 to 0.15625
- adapter_query_up: bfloat16 [256, 1536], replicated, may hold values from -1.5 to 1.5
- adapter_output_down: bfloat16 [1536, 256], replicated, may hold values from -0.15625 to 0.15625
- adapter_output_up: bfloat16 [256, 1536], replicated, may hold values from -1.5 to 1.5
- expert_norm_gain: bfloat16 [1536], replicated, may hold values from 0.099609375 to 1.8984375
- router: bfloat16 [1536, 8], replicated, may hold values from -0.15625 to 0.15625
- expert_gate_up: bfloat16 [8, 1536, 1536], P('exp'), may hold values from -0.15625 to 0.15625
- expert_down: bfloat16 [8, 768, 1536], P('exp'), may hold values from -0.21875 to 0.21875
Outputs:
- mixed_rows: bfloat16 [8192, 1536], P(('req', 'exp'))
The draws below stay inside these ranges and needn't reach their ends.
Inputs may be any that keep to these rules, and one draw needn't show every extreme that they name: `token_request_slot`: along a device's row the slots never fall; each of the 4 slots holds 1 to 128 tokens and one holds exactly 128. `prompt_page_table`: the entries whose index divided by 16 (rounded down) is p are the pages of prompt p in order; every page appears once. `routes`: each token names 4 different experts. Among the tokens of one device no expert is named more than 192 times, and in every draw some device's tokens name some expert exactly 192 times.
All inputs are finite; a program needn't handle non-finite values.
Results may differ from the reference program's by a relative error of at most 0.017.
The reference program's roundings to bfloat16 on the way count: a program that leaves them out, or rounds other values in their place, can miss the bound.
Values may be sent and summed in bfloat16 or wider, within the bound.
No kernel may reach another device: no remote copies, remote signals or barrier semaphores. Data moves between devices by JAX's collectives and lax.ppermute only.
A program may use at most 128 MiB of HBM per device.

```python
import math
import jax
import jax.numpy as jnp
import numpy as np
from jax import lax

MODEL_WIDTH = 1536
QUERY_HEADS = 12
KEY_VALUE_HEADS = 2
HEAD_WIDTH = 128
FFE = 768
TOPK = 4
ADAPTER_RANK = 16
ADAPTER_COUNT = 16
E = 8
TOK_DEV = 256
REQ_DEV = 4
SEGMOST = 128
PAGE_TOKENS = 16
PPP = 16
PROMPT_LENGTH = 256
PROMPTS = 8
CACHE_PAGES = 128
GROUPS = 32
TOKENS = 8192
REQUESTS = 128
CAP = 192


def draw_shared_prompt_cache(key, part):
    cache_layout = (CACHE_PAGES, PAGE_TOKENS, 2 * KEY_VALUE_HEADS * HEAD_WIDTH)
    values = jax.random.normal(key, cache_layout, jnp.float32)
    return jnp.clip(values, -6.0, 6.0).astype(jnp.bfloat16)


def set_ends(entries, rng, smallest, largest):
    shape = entries.shape
    place = [jax.random.randint(jax.random.fold_in(rng, axis), (), 0, shape[axis]) for axis in range(len(shape))]
    entries = entries.at[tuple(place)].set(smallest)
    longest = shape.index(max(shape))
    place[longest] = (place[longest] + 1) % shape[longest]
    return entries.at[tuple(place)].set(largest)


def shard_levels(key, dims, cuts, least, top_value):
    level = 1.0
    for dim, shards_of in cuts:
        heights = jax.random.uniform(jax.random.fold_in(jax.random.fold_in(key, 6), dim), (shards_of,), jnp.float32, least / len(cuts), top_value / len(cuts))
        level = level * jnp.repeat(jnp.exp(heights), dims[dim] // shards_of).reshape((-1,) + (1,) * (len(dims) - 1 - dim))
    return level


def length_profile(count, total, bound, lean):
    weights = [(1 << 20) // math.isqrt(rank ** lean) + 1 for rank in range(2, count + 1)]
    surplus, given = total - bound - (count - 1), [1] * (count - 1)
    while surplus > 0:
        candidates = [i for i in range(count - 1) if given[i] < bound]
        mass, remaining = sum([weights[i] for i in candidates]), surplus
        for i in candidates:
            addition = min(bound - given[i], max(1, remaining * weights[i] // mass), surplus)
            given[i] = given[i] + addition
            surplus = surplus - addition
    return np.array([bound] + given)


def ragged_sizes(key, amount, total, most, slope):
    if amount == 2:
        one = jax.random.randint(key, (), max(1, total - most), min(most, total - 1) + 1)
        return jnp.stack([one, total - one])
    lengths = jnp.asarray(length_profile(amount, total, most, slope), jnp.int32)
    twos = (amount - 1) // 2
    source_of, sink = lengths[1:1 + 2 * twos:2], lengths[2:2 + 2 * twos:2]
    room = jnp.minimum(source_of - 1, most - sink)
    passed = jax.random.randint(jax.random.fold_in(key, 1), (twos,), 0, 1 << 20) % (room + 1)
    lengths = lengths.at[1:1 + 2 * twos:2].set(source_of - passed).at[2:2 + 2 * twos:2].set(sink + passed)
    return lengths[jax.random.permutation(jax.random.fold_in(key, 2), amount)]


def routed_block(key, own, number, rows, number_of, top, bound, lean):
    ranking = jax.random.permutation(key, number_of)
    crowded, common = shares(number_of, rows * top, bound, lean, True), shares(number_of, rows * top, bound, lean, False)
    places = jnp.arange(number_of)

    def named(lengths, turn):
        used = int((lengths > 0).sum())
        fixed = max(1, used // 4)
        shifted = fixed + (places - fixed + turn * (used - fixed)) % max(1, number_of - fixed)
        return jnp.zeros((number_of,), jnp.int32).at[ranking[jnp.where(places < fixed, places, shifted)]].set(jnp.asarray(lengths, jnp.int32))

    lengths = jnp.where(number % 4 == 0, named(crowded, number // 4), named(common, number - number // 4 - 1))
    mixed = jax.random.permutation(jax.random.fold_in(own, 3), number_of)
    giver, receiver = mixed[0:number_of // 2 * 2:2], mixed[1:number_of // 2 * 2:2]
    room = jnp.minimum(lengths[giver] - 1, bound - lengths[receiver]) // 2
    room = jnp.where((giver == ranking[0]) | (receiver == ranking[0]) | (lengths[receiver] == 0), 0, jnp.maximum(room, 0))
    shifted = jax.random.randint(jax.random.fold_in(own, 4), (number_of // 2,), 0, 1 << 20) % (room + 1)
    lengths = lengths.at[giver].add(-shifted).at[receiver].add(shifted)
    members = jnp.searchsorted(jnp.cumsum(lengths), jnp.arange(rows * top), side="right").astype(jnp.int32)
    table = members.reshape(top, rows).T
    table = table[jax.random.permutation(jax.random.fold_in(own, 1), rows)]
    turn = jax.random.randint(jax.random.fold_in(own, 2), (rows, 1), 0, top)
    return jnp.take_along_axis(table, (jnp.arange(top)[None, :] + turn) % top, axis=1)


def shares(amount, total, reach, lean, full):
    portions = [(1 << 20) // math.isqrt(rank ** lean) + 1 for rank in range(1, amount + 1)]
    largest = reach if full else min(reach, max(-(-total // amount), total * portions[0] // sum(portions)))
    least = 1 if total - largest >= amount - 1 else 0
    given, surplus = [largest] + [least] * (amount - 1), total - largest - least * (amount - 1)
    while surplus > 0:
        candidates = [i for i in range(1, amount) if given[i] < largest] or [i for i in range(1, amount) if given[i] < reach]
        pool, remaining = sum([portions[i] for i in candidates]), surplus
        for i in candidates:
            more = min(reach - given[i], max(1, remaining * portions[i] // pool), surplus)
            given[i] = given[i] + more
            surplus = surplus - more
    return np.array(given)


def noise(own_key, extent, scale, limit, cuts=(), held_as=jnp.bfloat16):
    values = scale * jax.random.normal(own_key, extent, jnp.float32)
    if cuts:
        values = values * shard_levels(own_key, extent, cuts, -0.22, 0.18)
    return jnp.clip(values, -limit, limit).astype(held_as)


def setup_inputs(seed: int = 0) -> dict:
    key_of = jax.random.split(jax.random.key(seed), 20)
    tokens = noise(key_of[0], (TOKENS, MODEL_WIDTH), 1.0, 6.0, ((0, 32),))
    token_request_slot = jax.vmap(lambda own: jnp.searchsorted(jnp.cumsum(ragged_sizes(own, REQ_DEV, TOK_DEV, SEGMOST, 2)), jnp.arange(TOK_DEV), side="right"))(jax.random.split(key_of[1], GROUPS)).reshape((GROUPS, TOK_DEV)).astype(jnp.int32)
    request_prompt = set_ends(jax.random.randint(key_of[2], (REQUESTS,), 0, PROMPTS), jax.random.fold_in(key_of[2], 1), 0, PROMPTS - 1).astype(jnp.int32)
    request_adapter = set_ends(jax.random.randint(key_of[3], (REQUESTS,), 0, ADAPTER_COUNT), jax.random.fold_in(key_of[3], 1), 0, ADAPTER_COUNT - 1).astype(jnp.int32)
    prompt_page_table = jax.random.permutation(key_of[4], CACHE_PAGES).astype(jnp.int32)
    shared_prompt_cache = draw_shared_prompt_cache(jax.random.fold_in(key_of[19], 71), 0)
    routes_keys = jax.random.split(jax.random.fold_in(key_of[6], 1), TOKENS // TOK_DEV)
    routes_turns = jax.random.permutation(jax.random.fold_in(key_of[6], 3), TOKENS // TOK_DEV)
    routes = jax.vmap(lambda own, number: routed_block(jax.random.fold_in(key_of[6], 2), own, number, TOK_DEV, E, TOPK, CAP, 1))(routes_keys, routes_turns).reshape((TOKENS, TOPK))
    attention_norm_gain = jnp.clip(1.0 + 0.18 * jax.random.normal(key_of[7], (MODEL_WIDTH,), jnp.float32), 0.099609375, 1.8984375).astype(jnp.bfloat16)
    query_matrix = noise(key_of[8], (MODEL_WIDTH, QUERY_HEADS * HEAD_WIDTH), MODEL_WIDTH ** -0.5, 0.15625)
    key_value_weight = noise(key_of[9], (MODEL_WIDTH, 2 * KEY_VALUE_HEADS * HEAD_WIDTH), MODEL_WIDTH ** -0.5, 0.15625)
    attention_output_weight = noise(key_of[10], (QUERY_HEADS * HEAD_WIDTH, MODEL_WIDTH), (QUERY_HEADS * HEAD_WIDTH) ** -0.5, 0.15625)
    adapter_query_down = noise(key_of[11], (MODEL_WIDTH, ADAPTER_COUNT * ADAPTER_RANK), MODEL_WIDTH ** -0.5, 0.15625)
    adapter_query_up = noise(key_of[12], (ADAPTER_COUNT * ADAPTER_RANK, QUERY_HEADS * HEAD_WIDTH), ADAPTER_RANK ** -0.5, 1.5)
    adapter_output_down = noise(key_of[13], (QUERY_HEADS * HEAD_WIDTH, ADAPTER_COUNT * ADAPTER_RANK), (QUERY_HEADS * HEAD_WIDTH) ** -0.5, 0.15625)
    adapter_output_up = noise(key_of[14], (ADAPTER_COUNT * ADAPTER_RANK, MODEL_WIDTH), ADAPTER_RANK ** -0.5, 1.5)
    expert_norm_gain = jnp.clip(1.0 + 0.18 * jax.random.normal(key_of[15], (MODEL_WIDTH,), jnp.float32), 0.099609375, 1.8984375).astype(jnp.bfloat16)
    router = noise(key_of[16], (MODEL_WIDTH, E), MODEL_WIDTH ** -0.5, 0.15625)
    expert_gate_up = noise(key_of[17], (E, MODEL_WIDTH, 2 * FFE), MODEL_WIDTH ** -0.5, 0.15625, ((0, 8),))
    expert_down = noise(key_of[18], (E, FFE, MODEL_WIDTH), FFE ** -0.5, 0.21875, ((0, 8),))
    return dict(tokens=tokens, token_request_slot=token_request_slot, request_prompt=request_prompt, request_adapter=request_adapter, prompt_page_table=prompt_page_table, shared_prompt_cache=shared_prompt_cache, routes=routes, attention_norm_gain=attention_norm_gain, query_matrix=query_matrix, key_value_weight=key_value_weight, attention_output_weight=attention_output_weight, adapter_query_down=adapter_query_down, adapter_query_up=adapter_query_up, adapter_output_down=adapter_output_down, adapter_output_up=adapter_output_up, expert_norm_gain=expert_norm_gain, router=router, expert_gate_up=expert_gate_up, expert_down=expert_down)


EPSILON = 1e-06
THETA = 1000000.0
VERY_NEGATIVE = -1e+30

def rms_norm(weight_matrix, gain_vector):
    values = weight_matrix.astype(jnp.float32)
    factor = lax.rsqrt(lax.optimization_barrier(jnp.mean(values * values, axis=-1, keepdims=True)) + EPSILON)
    return (values * factor * gain_vector.astype(jnp.float32)).astype(jnp.bfloat16)

def apply_rotary(values, token_positions):
    half_width = values.shape[-1] // 2
    frequency = THETA ** (-jnp.arange(half_width).astype(jnp.float32) / half_width)
    angles = token_positions.astype(jnp.float32)[:, None] * frequency[None, :]
    cosine = jnp.cos(angles)[:, None, :]
    sine_table = jnp.sin(angles)[:, None, :]
    first_half = values[..., :half_width]
    second = values[..., half_width:]
    return jnp.concatenate([first_half * cosine - second * sine_table, second * cosine + first_half * sine_table], axis=-1)

def adapter_update(weight_matrix, down_proj, up_proj, token_adapter):
    inner = jnp.dot(weight_matrix, down_proj, preferred_element_type=jnp.float32)
    owner_slot = jnp.arange(down_proj.shape[1], dtype=jnp.int32) // ADAPTER_RANK
    inner = jnp.where(owner_slot[None, :] == token_adapter[:, None], inner, 0.0).astype(jnp.bfloat16)
    return jnp.dot(inner, up_proj, preferred_element_type=jnp.float32)

def request_info(request_row, prompt_req, adapter_req):
    new_token_count = request_row.shape[0]
    request_slot_count = prompt_req.shape[0]
    matches = request_row[:, None] == jnp.arange(request_slot_count, dtype=jnp.int32)[None, :]
    token_adapter = lax.optimization_barrier(jnp.sum(jnp.where(matches, adapter_req[None, :], 0), axis=1)).astype(jnp.int32)
    prompt_tok = lax.optimization_barrier(jnp.sum(jnp.where(matches, prompt_req[None, :], 0), axis=1)).astype(jnp.int32)
    token_index = jnp.arange(new_token_count, dtype=jnp.int32)
    first_row = lax.optimization_barrier(jnp.min(jnp.where(matches, token_index[:, None], new_token_count), axis=0)).astype(jnp.int32)
    start_tok = lax.optimization_barrier(jnp.sum(jnp.where(matches, first_row[None, :], 0), axis=1)).astype(jnp.int32)
    token_positions = (PROMPT_LENGTH + token_index - start_tok).astype(jnp.int32)
    return (token_adapter, prompt_tok, token_positions)

def apply_projection(tokens, token_adapter, token_positions, attention_norm_gain, query_matrix, key_value_weight, adapter_query_down, adapter_query_up):
    new_token_count = tokens.shape[0]
    normalized = rms_norm(tokens, attention_norm_gain)
    query_rows = jnp.dot(normalized, query_matrix, preferred_element_type=jnp.float32)
    query_rows = query_rows + adapter_update(normalized, adapter_query_down, adapter_query_up, token_adapter)
    query_rows = apply_rotary(query_rows.reshape(new_token_count, QUERY_HEADS, HEAD_WIDTH), token_positions).astype(jnp.bfloat16)
    key_value_rows = jnp.dot(normalized, key_value_weight, preferred_element_type=jnp.float32).reshape(new_token_count, 2 * KEY_VALUE_HEADS, HEAD_WIDTH)
    key_matrix = apply_rotary(key_value_rows[:, :KEY_VALUE_HEADS], token_positions).astype(jnp.bfloat16)
    value_matrix = key_value_rows[:, KEY_VALUE_HEADS:].astype(jnp.bfloat16)
    return (query_rows, key_matrix, value_matrix)

def finalize(attention_output, tokens, token_adapter, attention_output_weight, adapter_output_down, adapter_output_up):
    expert_mixture = jnp.dot(attention_output, attention_output_weight, preferred_element_type=jnp.float32)
    expert_mixture = expert_mixture + adapter_update(attention_output, adapter_output_down, adapter_output_up, token_adapter)
    return (tokens.astype(jnp.float32) + expert_mixture).astype(jnp.bfloat16)

def gate_weights(ffn_normed, router, routes):
    logits = jnp.dot(ffn_normed, router, preferred_element_type=jnp.float32)
    picked = jnp.take_along_axis(logits, routes, axis=1)
    squashed = jax.nn.sigmoid(picked)
    return squashed / lax.optimization_barrier(jnp.sum(squashed, axis=1, keepdims=True))

def slot_of(routes, experts, capacity):
    flat_routes = routes.reshape(-1)
    onehot = (flat_routes[:, None] == jnp.arange(experts, dtype=jnp.int32)[None, :]).astype(jnp.int32)
    before = (jnp.cumsum(onehot, axis=0) - onehot).astype(jnp.int32)
    rank_pick = lax.optimization_barrier(jnp.sum(before * onehot, axis=1)).astype(jnp.int32)
    return (flat_routes * capacity + rank_pick).astype(jnp.int32)

def device_attention(query_rows, key_matrix, value_matrix, request_row, prompt_req, prompt_page_table, shared_prompt_cache):
    new_token_count = query_rows.shape[0]
    request_slot_count = prompt_req.shape[0]
    table = prompt_page_table.reshape(-1, PPP)
    page_indices = jnp.take(table, prompt_req, axis=0).reshape(-1)
    page_token_rows = jnp.take(shared_prompt_cache, page_indices, axis=0).reshape(request_slot_count * PROMPT_LENGTH, 2 * KEY_VALUE_HEADS, HEAD_WIDTH)
    every_key = jnp.concatenate([page_token_rows[:, :KEY_VALUE_HEADS], key_matrix], axis=0).astype(jnp.float32)
    every_value = jnp.concatenate([page_token_rows[:, KEY_VALUE_HEADS:], value_matrix], axis=0).astype(jnp.float32)
    token_index = jnp.arange(new_token_count, dtype=jnp.int32)
    owner_slot = jnp.arange(request_slot_count * PROMPT_LENGTH, dtype=jnp.int32) // PROMPT_LENGTH
    prompt_valid_mask = request_row[:, None] == owner_slot[None, :]
    local_ok = (request_row[:, None] == request_row[None, :]) & (token_index[None, :] <= token_index[:, None])
    allowed = jnp.concatenate([prompt_valid_mask, local_ok], axis=1)
    grouped_queries = query_rows.reshape(new_token_count, KEY_VALUE_HEADS, QUERY_HEADS // KEY_VALUE_HEADS, HEAD_WIDTH).astype(jnp.float32)
    scores = jnp.einsum('tkgd,nkd->tkgn', grouped_queries, every_key) * HEAD_WIDTH ** (-0.5)
    scores = jnp.where(allowed[:, None, None, :], scores, VERY_NEGATIVE)
    running_max = lax.optimization_barrier(jnp.max(scores, axis=-1, keepdims=True))
    weights = jnp.exp(scores - running_max)
    totals = lax.optimization_barrier(jnp.sum(weights, axis=-1))
    rounded = lax.optimization_barrier(weights.astype(jnp.bfloat16))
    summed = jnp.einsum('tkgn,nkd->tkgd', rounded.astype(jnp.float32), every_value)
    return (summed / totals[..., None]).reshape(new_token_count, QUERY_HEADS * HEAD_WIDTH).astype(jnp.bfloat16)

def reference(tokens, token_request_slot, request_prompt, request_adapter, prompt_page_table, shared_prompt_cache, routes, attention_norm_gain, query_matrix, key_value_weight, attention_output_weight, adapter_query_down, adapter_query_up, adapter_output_down, adapter_output_up, expert_norm_gain, router, expert_gate_up, expert_down):
    groups = token_request_slot.shape[0]
    new_token_count = token_request_slot.shape[1]
    request_slot_count = request_prompt.shape[0] // groups
    width = tokens.shape[1]

    def one_device(inputs):
        weight_matrix, request_row, prompt_req, adapter_req = inputs
        token_adapter, prompt_tok, token_positions = request_info(request_row, prompt_req, adapter_req)
        query_rows, key_matrix, value_matrix = apply_projection(weight_matrix, token_adapter, token_positions, attention_norm_gain, query_matrix, key_value_weight, adapter_query_down, adapter_query_up)
        attention_output = device_attention(query_rows, key_matrix, value_matrix, request_row, prompt_req, prompt_page_table, shared_prompt_cache)
        return finalize(attention_output, weight_matrix, token_adapter, attention_output_weight, adapter_output_down, adapter_output_up)
    hidden_state = lax.map(one_device, (tokens.reshape(groups, new_token_count, width), token_request_slot, request_prompt.reshape(groups, request_slot_count), request_adapter.reshape(groups, request_slot_count)))
    hidden_state = hidden_state.reshape(groups * new_token_count, width)
    ffn_normed = rms_norm(hidden_state, expert_norm_gain)
    gates = gate_weights(ffn_normed, router, routes)
    experts = expert_gate_up.shape[0]
    destination = jax.vmap(lambda block: slot_of(block, experts, CAP))(routes.reshape(groups, new_token_count, TOPK))
    normed_dev = ffn_normed.reshape(groups, new_token_count, width)
    gates_dev = gates.reshape(groups, new_token_count * TOPK)
    device_line = jnp.arange(groups, dtype=jnp.int32)[:, None]
    source = jnp.broadcast_to(jnp.arange(new_token_count * TOPK, dtype=jnp.int32) // TOPK, (groups, new_token_count * TOPK))

    def one_expert(totals, inputs):
        weight_in, weight_out, number = inputs
        routed = destination // CAP == number
        slot_index = jnp.where(routed, destination % CAP, CAP).astype(jnp.int32)
        token_of = jnp.zeros((groups, CAP + 1), jnp.int32).at[device_line, slot_index].set(source)[:, :CAP]
        gate_of = jnp.zeros((groups, CAP + 1), jnp.float32).at[device_line, slot_index].set(gates_dev)[:, :CAP]
        filled = jnp.zeros((groups, CAP + 1), jnp.bool_).at[device_line, slot_index].set(routed)[:, :CAP]
        chosen = jnp.where(filled[..., None], normed_dev[device_line, token_of], jnp.zeros((), jnp.bfloat16))
        inner = jnp.dot(chosen.reshape(groups * CAP, width), weight_in, preferred_element_type=jnp.float32)
        units = (jax.nn.relu(inner[:, :FFE]) * inner[:, FFE:]).astype(jnp.bfloat16)
        result = jnp.dot(units, weight_out, preferred_element_type=jnp.float32).astype(jnp.bfloat16)
        result = result.reshape(groups, CAP, width)
        added = jnp.where(filled[..., None], gate_of[..., None] * result.astype(jnp.float32), 0.0)
        totals = totals.at[device_line, token_of].add(added)
        return (totals, None)
    initial = jnp.zeros((groups, new_token_count, width), jnp.float32)
    totals, unused = lax.scan(one_expert, initial, (expert_gate_up, expert_down, jnp.arange(experts, dtype=jnp.int32)))
    mixed_rows = hidden_state.reshape(groups, new_token_count, width).astype(jnp.float32) + totals
    return mixed_rows.reshape(groups * new_token_count, width).astype(jnp.bfloat16)
```

```python
import functools

import jax
import jax.numpy as jnp
from jax import lax
from jax.experimental import pallas as pl
from jax.experimental.pallas import tpu as pltpu
from jax.sharding import PartitionSpec as P

QUERY_HEADS = 12
KEY_VALUE_HEADS = 2
HEAD_WIDTH = 128
ADAPTER_RANK = 16
PPP = 16
PROMPT_LENGTH = 256
SEGMOST = 128
TILE = 64


EPSILON = 1e-06
LOG2_THETA = 19.931568569324174
VERY_NEGATIVE = -1e30
LOG2_E = 1.4426950408889634
MIB = 1 << 20

VMEM = pl.BlockSpec(memory_space=pltpu.VMEM)
SMEM = pl.BlockSpec(memory_space=pltpu.SMEM)
ANY = pl.BlockSpec(memory_space=pl.ANY)


def dot(one, other):
    return jnp.dot(one, other, preferred_element_type=jnp.float32)


def dot_transposed(one, other):
    return lax.dot_general(one, other, (((1,), (1,)), ((), ())), preferred_element_type=jnp.float32)


def rms_norm(values, gain):
    factor = lax.rsqrt(jnp.mean(values * values, axis=-1, keepdims=True) + EPSILON)
    return (values * factor * gain.astype(jnp.float32)).astype(jnp.bfloat16)


class Scalars:
    def __init__(self, ref, requests):
        self.starts = [ref[1 + slot] for slot in range(requests)]
        self.adapters = [ref[1 + requests + slot] for slot in range(requests)]
        self.place = lambda index: ref[1 + 2 * requests + index]

    def slot_of(self, row):
        return sum((row >= start).astype(jnp.int32) for start in self.starts[1:])


def prepare_kernel(
    pages_each, sizes, where, slots, prompts, adapters, page_table, numbers, outer
):
    requests = prompts.shape[0]
    exp_size, req_size = sizes
    exp, req = where[0], where[1]
    numbers[0] = exp
    held = slots[...]
    for slot in range(requests):
        numbers[1 + slot] = jnp.sum((held < slot).astype(jnp.int32))
        numbers[1 + requests + slot] = adapters[slot]

    def place(index, carry):
        page = page_table[prompts[index // PPP] * PPP + index % PPP]
        owner = page // pages_each
        apart = (owner % exp_size) ^ exp
        apart_req = (owner // exp_size) ^ req
        block = ((apart % 2) * req_size + apart_req) * (exp_size // 2) + apart // 2
        numbers[1 + 2 * requests + index] = block * pages_each + page % pages_each
        return carry

    lax.fori_loop(0, requests * PPP, place, 0)
    chip = exp // 2
    at_end = jnp.where((chip == 0) | (chip == 3), 1.0, 0.0)
    outer[...] = jnp.full(outer.shape, at_end, jnp.float32)


def by_slot(rows, starts, values):
    found = jnp.full(rows.shape, values[0], jnp.int32)
    for start, value in zip(starts[1:], values[1:]):
        found = jnp.where(rows >= start, value, found)
    return found


def own_columns(inner, adapter):
    column = lax.broadcasted_iota(jnp.int32, inner.shape, 1)
    return jnp.where(column // ADAPTER_RANK == adapter, inner, 0.0).astype(jnp.bfloat16)


def copies(pairs, semaphores):
    made = [
        pltpu.make_async_copy(source, target, semaphores.at[number])
        for number, (source, target) in enumerate(pairs)
    ]
    for copy in made:
        copy.start()
    return made


def projection_kernel(requests, routes_each, *refs):
    numbers, gain, tokens_there, query_matrix_there = refs[:4]
    key_value_weight_there, down_there, up_there = refs[4:7]
    blocks, refs = refs[7:-10], refs[-10:]
    query_rows, keys, values, named = refs[:4]
    tokens, query_matrix, key_value_weight, down, up, semaphores = refs[4:]
    chunks = query_matrix.shape[0]
    wide = query_matrix.shape[2]
    pairs = [
        (tokens_there, tokens),
        (key_value_weight_there, key_value_weight),
        (down_there, down),
        (up_there, up),
    ]
    for chunk in range(chunks):
        columns = pl.ds(chunk * wide, wide)
        pairs.append((query_matrix_there.at[:, columns], query_matrix.at[chunk]))
    got = copies(pairs, semaphores)
    scalars = Scalars(numbers, requests)
    count = tokens.shape[0]
    rows = lax.broadcasted_iota(jnp.int32, (count, 1), 0)
    adapter = by_slot(rows, scalars.starts, scalars.adapters)
    position = PROMPT_LENGTH + rows - by_slot(rows, scalars.starts, scalars.starts)
    lane = lax.broadcasted_iota(jnp.int32, (1, HEAD_WIDTH), 1) % (HEAD_WIDTH // 2)
    frequency = jnp.exp2(lane.astype(jnp.float32) * (-2.0 * LOG2_THETA / HEAD_WIDTH))
    angle = position.astype(jnp.float32) * frequency
    cosine, sine = jnp.cos(angle), jnp.sin(angle)
    lane = lax.broadcasted_iota(jnp.int32, angle.shape, 1)
    sine = jnp.where(lane < HEAD_WIDTH // 2, -sine, sine)

    def rotated(head):
        other = pltpu.roll(head, HEAD_WIDTH // 2, 1)
        return (head * cosine + other * sine).astype(jnp.bfloat16)

    named_rows = named.shape[1]
    expert = lax.broadcasted_iota(jnp.int32, (named.shape[2], named_rows), 0).astype(jnp.float32)
    for number, block in enumerate(blocks):
        page = block[block.shape[0] - 1].astype(jnp.float32)
        across = page.shape[1] // named_rows
        mentioned = jnp.zeros(expert.shape, jnp.float32)
        for k in range(routes_each):
            first = k % across * named_rows
            route = page[k // across : k // across + 1, first : first + named_rows]
            mentioned = jnp.where(expert == route, 1.0, mentioned)
        named[number] = mentioned.T
    got[0].wait()
    normed = rms_norm(tokens[...].astype(jnp.float32), gain[...][None, :])
    got[1].wait()
    key_value = dot(normed, key_value_weight[...])
    for head in range(KEY_VALUE_HEADS):
        lanes = slice(head * HEAD_WIDTH, (head + 1) * HEAD_WIDTH)
        keys[:, lanes] = rotated(key_value[:, lanes])
    values[...] = key_value[:, KEY_VALUE_HEADS * HEAD_WIDTH :].astype(jnp.bfloat16)
    got[2].wait()
    inner = own_columns(dot(normed, down[...]), adapter)
    got[3].wait()
    for chunk in range(chunks):
        got[4 + chunk].wait()
        first = chunk * wide
        part = dot(normed, query_matrix[chunk]) + dot(inner, up[:, first : first + wide])
        for head in range(wide // HEAD_WIDTH):
            lanes = slice(head * HEAD_WIDTH, (head + 1) * HEAD_WIDTH)
            query_rows[:, first + head * HEAD_WIDTH : first + (head + 1) * HEAD_WIDTH] = rotated(
                part[:, lanes]
            )


def fetch_kernel(requests, req_size, rows, *refs):
    numbers, gain, query_rows, keys, values, tokens = refs[:6]
    there = refs[6:13]
    parts = refs[13 : 13 + 2 * req_size]
    hidden, normed, prompt_rows, *held = refs[13 + 2 * req_size : -7]
    cache, attended, scratch, token_rows, part_semaphores, semaphores, token_semaphore = refs[-7:]
    pages = parts[0].shape[0]
    pairs = [
        (part, cache.at[pl.ds(number * pages, pages)]) for number, part in enumerate(parts)
    ]
    got_parts = copies(pairs, part_semaphores)
    got_tokens = copies([(tokens.at[pl.ds(0, rows)], token_rows)], token_semaphore)
    got = copies(list(zip(there, held)), semaphores)
    scalars = Scalars(numbers, requests)
    for copy in got_parts:
        copy.wait()

    def fetch(index, carry):
        prompt_rows[index] = cache[scalars.place(index)]
        return carry

    lax.fori_loop(0, requests * PPP, fetch, 0, unroll=4)
    attend(0, rows, scalars, query_rows, keys, values, prompt_rows, attended)
    for copy in got_tokens + got[:3]:
        copy.wait()
    project(0, scalars, gain, attended, token_rows, held[:3], hidden, normed, scratch)
    for copy in got[3:]:
        copy.wait()


def attention_kernel(requests, first_row, *refs):
    numbers, gain, query_rows, keys, values, tokens, prompt_rows, *weights = refs[:-6]
    hidden, normed, attended, scratch, token_rows, token_semaphore = refs[-6:]
    rows = token_rows.shape[0]
    got = copies([(tokens.at[pl.ds(first_row, rows)], token_rows)], token_semaphore)
    scalars = Scalars(numbers, requests)
    attend(first_row, rows, scalars, query_rows, keys, values, prompt_rows, attended)
    got[0].wait()
    project(first_row, scalars, gain, attended, token_rows, weights, hidden, normed, scratch)


def attend(first_row, count, scalars, query_rows, keys, values, prompt_rows, attended):
    starts = scalars.starts
    requests = len(starts)
    group = QUERY_HEADS // KEY_VALUE_HEADS
    factor = HEAD_WIDTH ** (-0.5) * LOG2_E
    for begin in range(first_row, first_row + count, TILE):
        end = begin + TILE
        window = max(0, begin - SEGMOST)
        rows = begin + lax.broadcasted_iota(jnp.int32, (TILE, 1), 0)
        columns = window + lax.broadcasted_iota(jnp.int32, (TILE, end - window), 1)
        row_slot = by_slot(rows, starts, list(range(requests)))
        row_start = by_slot(rows, starts, starts)
        blocked = jnp.where((columns >= row_start) & (columns <= rows), 0.0, VERY_NEGATIVE)
        blocked = jnp.concatenate([blocked] * group, axis=0)
        row_slot = jnp.concatenate([row_slot] * group, axis=0)
        lanes, value_lanes, grouped, state = [], [], [], []
        for head in range(KEY_VALUE_HEADS):
            lanes.append(slice(head * HEAD_WIDTH, (head + 1) * HEAD_WIDTH))
            place = KEY_VALUE_HEADS + head
            value_lanes.append(slice(place * HEAD_WIDTH, (place + 1) * HEAD_WIDTH))
            heads = range(head * group, (head + 1) * group)
            stacked = [query_rows[begin:end, h * HEAD_WIDTH : (h + 1) * HEAD_WIDTH] for h in heads]
            grouped.append(jnp.concatenate(stacked, axis=0))
        for head in range(KEY_VALUE_HEADS):
            scores = dot_transposed(grouped[head], keys[window:end, lanes[head]]) * factor + blocked
            largest = jnp.max(scores, axis=1, keepdims=True)
            weights = jnp.exp2(scores - largest)
            total = jnp.sum(weights, axis=1, keepdims=True)
            state.append(
                (largest, total, dot(weights.astype(jnp.bfloat16), values[window:end, lanes[head]]))
            )

        def add_prompt(slot, state):
            prompt_pages = prompt_rows[pl.ds(slot * PPP, PPP)]
            prompt = prompt_pages.reshape(PROMPT_LENGTH, prompt_pages.shape[-1])
            apart = jnp.where(row_slot == slot, 0.0, VERY_NEGATIVE)
            now = []
            for head in range(KEY_VALUE_HEADS):
                largest, total, summed = state[head]
                scores = dot_transposed(grouped[head], prompt[:, lanes[head]]) * factor + apart
                highest = jnp.maximum(largest, jnp.max(scores, axis=1, keepdims=True))
                weights = jnp.exp2(scores - highest)
                shrink = jnp.exp2(largest - highest)
                total = total * shrink + jnp.sum(weights, axis=1, keepdims=True)
                added = dot(weights.astype(jnp.bfloat16), prompt[:, value_lanes[head]])
                now.append((highest, total, summed * shrink + added))
            return tuple(now)

        state = lax.fori_loop(
            scalars.slot_of(begin), scalars.slot_of(end - 1) + 1, add_prompt, tuple(state)
        )
        for head in range(KEY_VALUE_HEADS):
            largest, total, summed = state[head]
            result = (summed / total).astype(jnp.bfloat16)
            for place in range(group):
                h = head * group + place
                attended[
                    begin - first_row : end - first_row, h * HEAD_WIDTH : (h + 1) * HEAD_WIDTH
                ] = result[place * TILE : (place + 1) * TILE]


def project(first_row, scalars, gain, attended, tokens, weights, hidden, normed, scratch):
    output_weight, down, up = weights
    count = tokens.shape[0]
    rows = first_row + lax.broadcasted_iota(jnp.int32, (count, 1), 0)
    adapter = by_slot(rows, scalars.starts, scalars.adapters)
    inner = own_columns(dot(attended[...], down[...]), adapter)
    width = tokens.shape[1]
    squares = jnp.zeros((count, 1), jnp.float32)
    for first in range(0, width, 512):
        columns = slice(first, first + 512)
        added = dot(attended[...], output_weight[:, columns]) + dot(inner, up[:, columns])
        part = (tokens[:, columns].astype(jnp.float32) + added).astype(jnp.bfloat16)
        hidden[:, columns] = part
        part = part.astype(jnp.float32)
        scratch[:, columns] = part
        squares = squares + jnp.sum(part * part, axis=1, keepdims=True)
    scale = lax.rsqrt(squares / width + EPSILON)
    wide = gain[...][None, :].astype(jnp.float32)
    normed[...] = (scratch[...] * scale * wide).astype(jnp.bfloat16)


def expert_kernel(plan, numbers, near, far, named, router, *refs):
    weights, (out, units) = refs[:4], refs[-2:]
    exp = numbers[0]
    chip = exp // 2
    use_near, owner, start = plan(chip)
    if use_near is None:
        rows = jnp.concatenate([near[...], far[...]], axis=0)
    else:
        rows = jnp.where(use_near, near[...], far[...])
    mentioned = named[chip ^ owner, pl.ds(start, rows.shape[0]), :]
    squashed = jnp.where(mentioned > 0.0, jax.nn.sigmoid(dot_transposed(rows, router[...])), 0.0)
    gates = squashed / jnp.sum(squashed, axis=1, keepdims=True)
    lane = lax.broadcasted_iota(jnp.int32, gates.shape, 1)
    hidden_units, width = weights[1].shape
    for number in range(2):
        gate_up = weights[2 * number]
        for first in range(0, hidden_units, 256):
            left = dot(rows, gate_up[:, first : first + 256])
            right = dot(rows, gate_up[:, hidden_units + first : hidden_units + first + 256])
            units[number, :, first : first + 256] = (jnp.maximum(left, 0.0) * right).astype(
                jnp.bfloat16
            )
    gate_columns = [
        jnp.sum(jnp.where(lane == (exp ^ number), gates, 0.0), axis=1, keepdims=True)
        for number in range(2)
    ]
    for first in range(0, width, 512):
        columns = slice(first, first + 512)
        total = 0.0
        for number in range(2):
            result = dot(units[number], weights[2 * number + 1][:, columns]).astype(jnp.bfloat16)
            total = total + gate_columns[number] * result.astype(jnp.float32)
        out[:, columns] = total.astype(out.dtype)


def call(kernel, inputs, specs, outs, scratch, name, flops, limit, out_specs=None):
    moved = sum(x.size * x.dtype.itemsize for x in inputs)
    return pl.pallas_call(
        kernel,
        in_specs=specs,
        out_specs=out_specs or [VMEM] * len(outs),
        out_shape=outs,
        scratch_shapes=scratch,
        name=name,
        cost_estimate=pl.CostEstimate(flops=flops, bytes_accessed=moved, transcendentals=0),
        compiler_params=pltpu.CompilerParams(vmem_limit_bytes=limit * MIB),
    )(*inputs)


def expert_sum(near, far, plan, shared, dtype, rows=None, earlier=()):
    numbers, named, router, weights = shared
    rows = near.shape[0] if rows is None else rows
    hidden_units, width = weights[1].shape
    return call(
        functools.partial(expert_kernel, plan),
        [numbers, near, far, named, router, *weights, *earlier],
        [SMEM] + [VMEM] * 8 + [ANY] * len(earlier),
        [jax.ShapeDtypeStruct((rows, width), dtype)],
        [pltpu.VMEM((2, rows, hidden_units), jnp.bfloat16)],
        "expert_sum",
        12 * rows * width * hidden_units,
        10,
    )[0]


def after(values, *earlier):
    return pl.pallas_call(
        lambda *refs: None,
        in_specs=[ANY] * (len(values) + len(earlier)),
        out_specs=[ANY] * len(values),
        out_shape=[jax.ShapeDtypeStruct(x.shape, x.dtype) for x in values],
        input_output_aliases={number: number for number in range(len(values))},
        name="after",
        compiler_params=pltpu.CompilerParams(vmem_limit_bytes=MIB),
    )(*values, *earlier)


def chosen_kernel(outer, for_outer, for_inner, *refs):
    refs[-1][...] = jnp.where(outer[0:1, 0:1] > 0.0, for_outer[...], for_inner[...])


def added_kernel(one, other, *refs):
    total = one[...].astype(jnp.float32) + other[...].astype(jnp.float32)
    refs[-1][...] = total.astype(jnp.bfloat16)


def payload(kernel, inputs, earlier):
    one = inputs[-1]
    return call(
        kernel,
        [*inputs, *earlier],
        [VMEM] * len(inputs) + [ANY] * len(earlier),
        [jax.ShapeDtypeStruct(one.shape, one.dtype)],
        [],
        "payload",
        one.size,
        2,
    )[0]


def swap(values, axis, distance):
    size = lax.axis_size(axis)
    return lax.ppermute(values, axis, [(i, i ^ distance) for i in range(size)])


def gather_line(values):
    chips = lax.axis_size("exp") // 2
    return [values] + [swap(values, "exp", 2 * distance) for distance in range(1, chips)]


def gather_plane(line):
    return [swap(line, "req", distance) for distance in range(1, lax.axis_size("req"))]


def next_chip(values):
    size = lax.axis_size("exp")
    return lax.ppermute(values, "exp", [(i, (i + 2) % size) for i in range(size)])


def ring_experts(halves, shared, outer_here):
    chips = lax.axis_size("exp") // 2
    own = jnp.concatenate(halves, axis=0)
    rows, partial = own, None
    for step in range(1, chips):
        rows = next_chip(rows)
        plan = lambda chip, step=step: (True, lax.rem(chip + (chips - step), chips), 0)
        part = expert_sum(rows, rows, plan, shared, jnp.float32)
        if partial is not None:
            part = part + next_chip(partial).astype(jnp.float32)
        partial = part.astype(jnp.bfloat16)
    total = expert_sum(own, own, lambda chip: (True, chip, 0), shared, jnp.float32)
    if partial is not None:
        total = total + next_chip(partial).astype(jnp.float32)
    return total


COMPUTED = {
    2: ((1, 2, 1, 2), (0, 0, 0, 0)),
    3: ((2, 3, 0, 1), (0, 0, 0, 0)),
    4: ((3, 3, 0, 0), (0, 1, 1, 0)),
    5: ((3, 2, 1, 0), (1, 1, 1, 1)),
    6: ((2, 0, 3, 1), (1, 0, 0, 1)),
    7: ((1, 0, 3, 2), (1, 1, 1, 1)),
}


def by_chip(chip, numbers):
    found = numbers[0]
    for other, number in enumerate(numbers[1:], 1):
        found = jnp.where(chip == other, number, found)
    return found


def line_experts(halves, shared, outer_here):
    size = lax.axis_size("exp")
    first, second = halves
    half = first.shape[0]
    inner_pairs = [(i, i ^ 6) for i in range(2, size - 2)]

    def chosen(for_outer, for_inner, *earlier):
        return payload(chosen_kernel, [outer_here, for_outer, for_inner], earlier)

    def added(one, other, *earlier):
        return payload(added_kernel, [one, other], earlier)

    side, middle, sums = {}, {}, {}

    def send_side(slot, *earlier):
        if slot == 2:
            rows = chosen(second, middle[1], *earlier)
        elif slot <= 5:
            rows = chosen(sums[slot - 1], middle[slot - 1], *earlier)
        elif slot == 6:
            rows = chosen(sums[5], second, middle[5], *earlier)
        else:
            rows = added(middle[slot - 1], sums[slot - 1], *earlier)
        side[slot] = swap(rows, "exp", 2)
        return rows

    def send_middle(slot, *earlier):
        if slot <= 3:
            rows = chosen(side[slot - 1], side[slot - 1], *earlier)
        elif slot == 4:
            rows = chosen(side[3], second, *earlier)
        else:
            rows = added(side[slot - 1], sums[slot - 3], *earlier)
        middle[slot] = lax.ppermute(rows, "exp", inner_pairs)
        return rows

    side[1] = swap(first, "exp", 2)
    middle[1] = lax.ppermute(first, "exp", inner_pairs)
    last = second
    for slot in range(2, 9):
        if slot % 2:
            sent = send_middle(slot, send_side(slot, last))
        else:
            sent = send_side(slot, send_middle(slot, last))
        if slot in COMPUTED:
            inner_rows = middle[slot - 1] if slot <= 5 else side[slot - 5]

            def plan(chip, slot=slot):
                owners, whichs = COMPUTED[slot]
                use_near = (chip == 0) | (chip == 3)
                start = pl.multiple_of(by_chip(chip, whichs) * half, half)
                return use_near, by_chip(chip, owners), start

            sums[slot] = expert_sum(side[slot - 1], inner_rows, plan, shared, jnp.bfloat16)
            last = sums[slot]
    plan = lambda chip: (None, chip, 0)
    total = expert_sum(first, second, plan, shared, jnp.float32, 2 * half, (sent,))
    back = chosen(side[7], side[3]).astype(jnp.float32) + middle[5].astype(jnp.float32)
    back_second = side[8].astype(jnp.float32) + middle[8].astype(jnp.float32)
    return total + jnp.concatenate([back, back_second], axis=0)


def on_device(
    tokens,
    token_request_slot,
    request_prompt,
    request_adapter,
    prompt_page_table,
    shared_prompt_cache,
    routes,
    attention_norm_gain,
    query_matrix,
    key_value_weight,
    attention_output_weight,
    adapter_query_down,
    adapter_query_up,
    adapter_output_down,
    adapter_output_up,
    expert_norm_gain,
    router,
    expert_gate_up,
    expert_down,
):
    count, width = tokens.shape
    requests = request_prompt.shape[0]
    experts = router.shape[1]
    other_gate_up = swap(expert_gate_up, "exp", 1)
    other_down = swap(expert_down, "exp", 1)
    page = shared_prompt_cache.shape[1:]
    pages_each = shared_prompt_cache.shape[0]
    where = jnp.stack([lax.axis_index("exp"), lax.axis_index("req")]).astype(jnp.int32)
    sizes = (lax.axis_size("exp"), lax.axis_size("req"))
    numbers, outer_here = call(
        functools.partial(prepare_kernel, pages_each, sizes),
        [where, token_request_slot, request_prompt, request_adapter, prompt_page_table],
        [SMEM, VMEM, SMEM, SMEM, SMEM],
        [
            jax.ShapeDtypeStruct((1 + 2 * requests + requests * PPP,), jnp.int32),
            jax.ShapeDtypeStruct((8, HEAD_WIDTH), jnp.float32),
        ],
        [],
        "prepare",
        count * width,
        4,
        [SMEM, VMEM],
    )
    route_rows = routes.T.reshape(-1, page[1]).astype(jnp.bfloat16)
    route_page = jnp.pad(route_rows, ((0, page[0] - route_rows.shape[0]), (0, 0)))
    blocks = gather_line(jnp.concatenate([shared_prompt_cache, route_page[None]], axis=0))
    line = jnp.concatenate([block[:pages_each] for block in blocks], axis=0)
    (line,) = after([line], outer_here)
    key_width = KEY_VALUE_HEADS * HEAD_WIDTH
    heads_width = query_matrix.shape[1]
    rank = adapter_query_down.shape[1]
    bfloat = lambda *shape: pltpu.VMEM(shape, jnp.bfloat16)
    query_rows, keys, values, named = call(
        functools.partial(projection_kernel, requests, routes.shape[1]),
        [
            numbers,
            attention_norm_gain,
            tokens,
            query_matrix,
            key_value_weight,
            adapter_query_down,
            adapter_query_up,
            *blocks,
        ],
        [SMEM, VMEM] + [ANY] * 5 + [VMEM] * len(blocks),
        [
            jax.ShapeDtypeStruct((count, columns), jnp.bfloat16)
            for columns in (heads_width, key_width, key_width)
        ]
        + [jax.ShapeDtypeStruct((len(blocks), count, experts), jnp.float32)],
        [
            bfloat(count, width),
            bfloat(heads_width // 512, width, 512),
            bfloat(width, 2 * key_width),
            bfloat(width, rank),
            bfloat(rank, heads_width),
            pltpu.SemaphoreType.DMA((4 + heads_width // 512,)),
        ],
        "projections",
        2 * count * width * (heads_width + 3 * key_width),
        52,
    )
    parts = after([line, *gather_plane(line)], keys)
    parts = [*parts] + [swap(part, "exp", 1) for part in parts]
    pages = len(parts) * parts[0].shape[0]
    half = count // 2
    rows_out = [jax.ShapeDtypeStruct((half, width), jnp.bfloat16)] * 2
    projected = [numbers, expert_norm_gain, query_rows, keys, values, tokens]
    output_weights = [attention_output_weight, adapter_output_down, adapter_output_up]
    weights = [expert_gate_up[0], expert_down[0], other_gate_up[0], other_down[0]]
    working = [
        bfloat(half, heads_width),
        pltpu.VMEM((half, width), jnp.float32),
        bfloat(half, width),
    ]
    hidden_first, first, prompt_rows, *held = call(
        functools.partial(fetch_kernel, requests, sizes[1], half),
        [*projected, *output_weights, *weights, *parts],
        [SMEM] + [VMEM] * 4 + [ANY] * (8 + len(parts)),
        rows_out
        + [bfloat(requests * PPP, *page)]
        + [bfloat(*weight.shape) for weight in output_weights + weights],
        [bfloat(pages, *page)]
        + working
        + [pltpu.SemaphoreType.DMA((number,)) for number in (len(parts), 7, 1)],
        "first_attention",
        2 * count * width * width,
        22,
    )
    hidden_second, second = call(
        functools.partial(attention_kernel, requests, half),
        [*projected, prompt_rows, *held[:3]],
        [SMEM] + [VMEM] * 4 + [ANY] + [VMEM] * 4,
        rows_out,
        working + [pltpu.SemaphoreType.DMA((1,))],
        "second_attention",
        2 * count * width * width,
        8,
    )
    hidden_state = jnp.concatenate([hidden_first, hidden_second], axis=0)
    halves, weights = (first, second), held[3:]
    experts_of = line_experts if lax.axis_size("exp") == 8 else ring_experts
    shared = (numbers, named, router.T, weights)
    mixed_rows = hidden_state.astype(jnp.float32) + experts_of(halves, shared, outer_here)
    return mixed_rows.astype(jnp.bfloat16)


def solution(mesh):
    return jax.shard_map(
        on_device,
        mesh=mesh,
        in_specs=(
            P(("req", "exp"), None),
            P(("req", "exp"), None),
            P(("req", "exp")),
            P(("req", "exp")),
            P(),
            P(("req", "exp"), None, None),
            P(("req", "exp"), None),
            P(),
            P(),
            P(),
            P(),
            P(),
            P(),
            P(),
            P(),
            P(),
            P(),
            P("exp", None, None),
            P("exp", None, None),
        ),
        out_specs=P(("req", "exp"), None),
        check_vma=False,
    )
```

```python
import functools

import jax
import jax.numpy as jnp
from jax import lax
from jax.experimental import pallas as pl
from jax.experimental.pallas import tpu as pltpu
from jax.sharding import PartitionSpec as P

QUERY_HEADS = 12
KEY_VALUE_HEADS = 2
HEAD_WIDTH = 128
ADAPTER_RANK = 16
PPP = 16
PROMPT_LENGTH = 256
SEGMOST = 128
TILE = 64


EPSILON = 1e-06
LOG2_THETA = 19.931568569324174
VERY_NEGATIVE = -1e30
LOG2_E = 1.4426950408889634
MIB = 1 << 20

VMEM = pl.BlockSpec(memory_space=pltpu.VMEM)
SMEM = pl.BlockSpec(memory_space=pltpu.SMEM)
ANY = pl.BlockSpec(memory_space=pl.ANY)


def dot(one, other):
    return jnp.dot(one, other, preferred_element_type=jnp.float32)


def dot_transposed(one, other):
    return lax.dot_general(one, other, (((1,), (1,)), ((), ())), preferred_element_type=jnp.float32)


def rms_norm(values, gain):
    factor = lax.rsqrt(jnp.mean(values * values, axis=-1, keepdims=True) + EPSILON)
    return (values * factor * gain.astype(jnp.float32)).astype(jnp.bfloat16)


class Scalars:
    def __init__(self, ref, requests):
        self.starts = [ref[1 + slot] for slot in range(requests)]
        self.adapters = [ref[1 + requests + slot] for slot in range(requests)]
        self.place = lambda index: ref[1 + 2 * requests + index]

    def slot_of(self, row):
        return sum((row >= start).astype(jnp.int32) for start in self.starts[1:])


def prepare_kernel(
    pages_each, sizes, where, slots, prompts, adapters, page_table, numbers, outer
):
    requests = prompts.shape[0]
    exp_size, req_size = sizes
    exp, req = where[0], where[1]
    numbers[0] = exp
    held = slots[...]
    for slot in range(requests):
        numbers[1 + slot] = jnp.sum((held < slot).astype(jnp.int32))
        numbers[1 + requests + slot] = adapters[slot]

    def place(index, carry):
        page = page_table[prompts[index // PPP] * PPP + index % PPP]
        owner = lax.div(page, pages_each)
        apart = lax.rem(owner, exp_size) ^ exp
        apart_req = lax.div(owner, exp_size) ^ req
        block = ((apart & 1) * req_size + apart_req) * (exp_size // 2) + (apart >> 1)
        numbers[1 + 2 * requests + index] = block * pages_each + lax.rem(page, pages_each)
        return carry

    lax.fori_loop(0, requests * PPP, place, 0)
    chip = exp // 2
    at_end = jnp.where((chip == 0) | (chip == 3), 1.0, 0.0)
    outer[...] = jnp.full(outer.shape, at_end, jnp.float32)


def by_slot(rows, starts, values):
    found = jnp.full(rows.shape, values[0], jnp.int32)
    for start, value in zip(starts[1:], values[1:]):
        found = jnp.where(rows >= start, value, found)
    return found


def own_columns(inner, adapter):
    column = lax.broadcasted_iota(jnp.int32, inner.shape, 1)
    return jnp.where(column // ADAPTER_RANK == adapter, inner, 0.0).astype(jnp.bfloat16)


def copies(pairs, semaphores):
    made = [
        pltpu.make_async_copy(source, target, semaphores.at[number])
        for number, (source, target) in enumerate(pairs)
    ]
    for copy in made:
        copy.start()
    return made


def projection_kernel(requests, routes_each, *refs):
    numbers, gain, tokens_there, query_matrix_there = refs[:4]
    key_value_weight_there, down_there, up_there = refs[4:7]
    blocks, refs = refs[7:-10], refs[-10:]
    query_rows, keys, values, named = refs[:4]
    tokens, query_matrix, key_value_weight, down, up, semaphores = refs[4:]
    chunks = query_matrix.shape[0]
    wide = query_matrix.shape[2]
    pairs = [
        (tokens_there, tokens),
        (key_value_weight_there, key_value_weight),
        (down_there, down),
        (up_there, up),
    ]
    for chunk in range(chunks):
        columns = pl.ds(chunk * wide, wide)
        pairs.append((query_matrix_there.at[:, columns], query_matrix.at[chunk]))
    got = copies(pairs, semaphores)
    scalars = Scalars(numbers, requests)
    count = tokens.shape[0]
    rows = lax.broadcasted_iota(jnp.int32, (count, 1), 0)
    adapter = by_slot(rows, scalars.starts, scalars.adapters)
    position = PROMPT_LENGTH + rows - by_slot(rows, scalars.starts, scalars.starts)
    lane = lax.broadcasted_iota(jnp.int32, (1, HEAD_WIDTH), 1) % (HEAD_WIDTH // 2)
    frequency = jnp.exp2(lane.astype(jnp.float32) * (-2.0 * LOG2_THETA / HEAD_WIDTH))
    angle = position.astype(jnp.float32) * frequency
    cosine, sine = jnp.cos(angle), jnp.sin(angle)
    lane = lax.broadcasted_iota(jnp.int32, angle.shape, 1)
    sine = jnp.where(lane < HEAD_WIDTH // 2, -sine, sine)

    def rotated(head):
        other = pltpu.roll(head, HEAD_WIDTH // 2, 1)
        return (head * cosine + other * sine).astype(jnp.bfloat16)

    named_rows = named.shape[1]
    expert = lax.broadcasted_iota(jnp.int32, (named.shape[2], named_rows), 0).astype(jnp.float32)
    for number, block in enumerate(blocks):
        page = block[block.shape[0] - 1].astype(jnp.float32)
        across = page.shape[1] // named_rows
        mentioned = jnp.zeros(expert.shape, jnp.float32)
        for k in range(routes_each):
            first = k % across * named_rows
            route = page[k // across : k // across + 1, first : first + named_rows]
            mentioned = jnp.where(expert == route, 1.0, mentioned)
        named[number] = mentioned.T
    got[0].wait()
    normed = rms_norm(tokens[...].astype(jnp.float32), gain[...][None, :])
    got[1].wait()
    key_value = dot(normed, key_value_weight[...])
    for head in range(KEY_VALUE_HEADS):
        lanes = slice(head * HEAD_WIDTH, (head + 1) * HEAD_WIDTH)
        keys[:, lanes] = rotated(key_value[:, lanes])
    values[...] = key_value[:, KEY_VALUE_HEADS * HEAD_WIDTH :].astype(jnp.bfloat16)
    got[2].wait()
    inner = own_columns(dot(normed, down[...]), adapter)
    got[3].wait()
    for chunk in range(chunks):
        got[4 + chunk].wait()
        first = chunk * wide
        part = dot(normed, query_matrix[chunk]) + dot(inner, up[:, first : first + wide])
        for head in range(wide // HEAD_WIDTH):
            lanes = slice(head * HEAD_WIDTH, (head + 1) * HEAD_WIDTH)
            query_rows[:, first + head * HEAD_WIDTH : first + (head + 1) * HEAD_WIDTH] = rotated(
                part[:, lanes]
            )


def fetch_kernel(requests, req_size, rows, *refs):
    numbers, gain, query_rows, keys, values, tokens = refs[:6]
    there = refs[6:13]
    parts = refs[13 : 13 + 2 * req_size]
    hidden, normed, prompt_rows, *held = refs[13 + 2 * req_size : -7]
    cache, attended, scratch, token_rows, part_semaphores, semaphores, token_semaphore = refs[-7:]
    pages = parts[0].shape[0]
    pairs = [
        (part, cache.at[pl.ds(number * pages, pages)]) for number, part in enumerate(parts)
    ]
    got_parts = copies(pairs, part_semaphores)
    got_tokens = copies([(tokens.at[pl.ds(0, rows)], token_rows)], token_semaphore)
    got = copies(list(zip(there, held)), semaphores)
    scalars = Scalars(numbers, requests)

    def fetch(index, carry):
        prompt_rows[index] = cache[scalars.place(index)]
        return carry

    def fetch_pages():
        for copy in got_parts:
            copy.wait()
        lax.fori_loop(0, requests * PPP, fetch, 0, unroll=4)

    attend(0, rows, scalars, query_rows, keys, values, prompt_rows, attended, fetch_pages)
    for copy in got_tokens + got[:3]:
        copy.wait()
    project(0, scalars, gain, attended, token_rows, held[:3], hidden, normed, scratch)
    for copy in got[3:]:
        copy.wait()


def attention_kernel(requests, first_row, *refs):
    numbers, gain, query_rows, keys, values, tokens, prompt_rows, *weights = refs[:-6]
    hidden, normed, attended, scratch, token_rows, token_semaphore = refs[-6:]
    rows = token_rows.shape[0]
    got = copies([(tokens.at[pl.ds(first_row, rows)], token_rows)], token_semaphore)
    scalars = Scalars(numbers, requests)
    attend(first_row, rows, scalars, query_rows, keys, values, prompt_rows, attended)
    got[0].wait()
    project(first_row, scalars, gain, attended, token_rows, weights, hidden, normed, scratch)


def attend(
    first_row, count, scalars, query_rows, keys, values, prompt_rows, attended, then=lambda: None
):
    starts = scalars.starts
    requests = len(starts)
    group = QUERY_HEADS // KEY_VALUE_HEADS
    factor = HEAD_WIDTH ** (-0.5) * LOG2_E
    tiles = []
    for begin in range(first_row, first_row + count, TILE):
        end = begin + TILE
        window = max(0, begin - SEGMOST)
        rows = begin + lax.broadcasted_iota(jnp.int32, (TILE, 1), 0)
        columns = window + lax.broadcasted_iota(jnp.int32, (TILE, end - window), 1)
        row_slot = by_slot(rows, starts, list(range(requests)))
        row_start = by_slot(rows, starts, starts)
        blocked = jnp.where((columns >= row_start) & (columns <= rows), 0.0, VERY_NEGATIVE)
        blocked = jnp.concatenate([blocked] * group, axis=0)
        row_slot = jnp.concatenate([row_slot] * group, axis=0)
        lanes, value_lanes, grouped, state = [], [], [], []
        for head in range(KEY_VALUE_HEADS):
            lanes.append(slice(head * HEAD_WIDTH, (head + 1) * HEAD_WIDTH))
            place = KEY_VALUE_HEADS + head
            value_lanes.append(slice(place * HEAD_WIDTH, (place + 1) * HEAD_WIDTH))
            heads = range(head * group, (head + 1) * group)
            stacked = [query_rows[begin:end, h * HEAD_WIDTH : (h + 1) * HEAD_WIDTH] for h in heads]
            grouped.append(jnp.concatenate(stacked, axis=0))
        for head in range(KEY_VALUE_HEADS):
            scores = dot_transposed(grouped[head], keys[window:end, lanes[head]]) * factor + blocked
            largest = jnp.max(scores, axis=1, keepdims=True)
            weights = jnp.exp2(scores - largest)
            total = jnp.sum(weights, axis=1, keepdims=True)
            state.append(
                (largest, total, dot(weights.astype(jnp.bfloat16), values[window:end, lanes[head]]))
            )
        tiles.append((begin, end, row_slot, grouped, state))
    then()
    for begin, end, row_slot, grouped, state in tiles:

        def add_prompt(slot, state, row_slot=row_slot, grouped=grouped):
            prompt_pages = prompt_rows[pl.ds(slot * PPP, PPP)]
            prompt = prompt_pages.reshape(PROMPT_LENGTH, prompt_pages.shape[-1])
            apart = jnp.where(row_slot == slot, 0.0, VERY_NEGATIVE)
            now = []
            for head in range(KEY_VALUE_HEADS):
                largest, total, summed = state[head]
                scores = dot_transposed(grouped[head], prompt[:, lanes[head]]) * factor + apart
                highest = jnp.maximum(largest, jnp.max(scores, axis=1, keepdims=True))
                weights = jnp.exp2(scores - highest)
                shrink = jnp.exp2(largest - highest)
                total = total * shrink + jnp.sum(weights, axis=1, keepdims=True)
                added = dot(weights.astype(jnp.bfloat16), prompt[:, value_lanes[head]])
                now.append((highest, total, summed * shrink + added))
            return tuple(now)

        state = lax.fori_loop(
            scalars.slot_of(begin), scalars.slot_of(end - 1) + 1, add_prompt, tuple(state)
        )
        for head in range(KEY_VALUE_HEADS):
            largest, total, summed = state[head]
            result = (summed / total).astype(jnp.bfloat16)
            for place in range(group):
                h = head * group + place
                attended[
                    begin - first_row : end - first_row, h * HEAD_WIDTH : (h + 1) * HEAD_WIDTH
                ] = result[place * TILE : (place + 1) * TILE]


def project(first_row, scalars, gain, attended, tokens, weights, hidden, normed, scratch):
    output_weight, down, up = weights
    count = tokens.shape[0]
    rows = first_row + lax.broadcasted_iota(jnp.int32, (count, 1), 0)
    adapter = by_slot(rows, scalars.starts, scalars.adapters)
    inner = own_columns(dot(attended[...], down[...]), adapter)
    width = tokens.shape[1]
    squares = jnp.zeros((count, 1), jnp.float32)
    for first in range(0, width, 512):
        columns = slice(first, first + 512)
        added = dot(attended[...], output_weight[:, columns]) + dot(inner, up[:, columns])
        part = (tokens[:, columns].astype(jnp.float32) + added).astype(jnp.bfloat16)
        hidden[:, columns] = part
        part = part.astype(jnp.float32)
        scratch[:, columns] = part
        squares = squares + jnp.sum(part * part, axis=1, keepdims=True)
    scale = lax.rsqrt(squares / width + EPSILON)
    wide = gain[...][None, :].astype(jnp.float32)
    normed[...] = (scratch[...] * scale * wide).astype(jnp.bfloat16)


def gated_experts(exp, rows, mentioned, router, weights, units):
    squashed = jnp.where(mentioned > 0.0, jax.nn.sigmoid(dot_transposed(rows, router[...])), 0.0)
    gates = squashed / jnp.sum(squashed, axis=1, keepdims=True)
    lane = lax.broadcasted_iota(jnp.int32, gates.shape, 1)
    hidden_units, width = weights[1].shape
    for number in range(2):
        gate_up = weights[2 * number]
        for first in range(0, hidden_units, 256):
            left = dot(rows, gate_up[:, first : first + 256])
            right = dot(rows, gate_up[:, hidden_units + first : hidden_units + first + 256])
            units[number, :, first : first + 256] = (jnp.maximum(left, 0.0) * right).astype(
                jnp.bfloat16
            )
    gate_columns = [
        jnp.sum(jnp.where(lane == (exp ^ number), gates, 0.0), axis=1, keepdims=True)
        for number in range(2)
    ]
    for first in range(0, width, 512):
        columns = slice(first, first + 512)
        total = 0.0
        for number in range(2):
            result = dot(units[number], weights[2 * number + 1][:, columns]).astype(jnp.bfloat16)
            total = total + gate_columns[number] * result.astype(jnp.float32)
        yield columns, total


def expert_kernel(plan, numbers, near, far, named, router, *refs):
    weights, (out, units) = refs[:4], refs[4:]
    exp = numbers[0]
    chip = exp // 2
    use_near, owner, start = plan(chip)
    rows = jnp.where(use_near, near[...], far[...])
    mentioned = named[chip ^ owner, pl.ds(start, rows.shape[0]), :]
    for columns, total in gated_experts(exp, rows, mentioned, router, weights, units):
        out[:, columns] = total.astype(out.dtype)


def own_kernel(numbers, first, second, named, router, *refs):
    weights, refs = refs[:4], refs[4:]
    hidden_first, hidden_second, back, other_back = refs[:4]
    out_first, out_second, units = refs[-3:]
    rows = jnp.concatenate([first[...], second[...]], axis=0)
    half = first.shape[0]
    for columns, total in gated_experts(numbers[0], rows, named[0], router, weights, units):
        came = back[:, columns].astype(jnp.float32) + other_back[:, columns].astype(jnp.float32)
        upper = hidden_first[:, columns].astype(jnp.float32) + total[:half] + came
        out_first[:, columns] = upper.astype(jnp.bfloat16)
        out_second[:, columns] = hidden_second[:, columns].astype(jnp.float32) + total[half:]


def call(kernel, inputs, specs, outs, scratch, name, flops, limit, out_specs=None):
    moved = sum(x.size * x.dtype.itemsize for x in inputs)
    return pl.pallas_call(
        kernel,
        in_specs=specs,
        out_specs=out_specs or [VMEM] * len(outs),
        out_shape=outs,
        scratch_shapes=scratch,
        name=name,
        cost_estimate=pl.CostEstimate(flops=flops, bytes_accessed=moved, transcendentals=0),
        compiler_params=pltpu.CompilerParams(vmem_limit_bytes=limit * MIB),
    )(*inputs)


def expert_sum(near, far, plan, shared, dtype):
    numbers, named, router, weights = shared
    rows = near.shape[0]
    hidden_units, width = weights[1].shape
    return call(
        functools.partial(expert_kernel, plan),
        [numbers, near, far, named, router, *weights],
        [SMEM] + [VMEM] * 8,
        [jax.ShapeDtypeStruct((rows, width), dtype)],
        [pltpu.VMEM((2, rows, hidden_units), jnp.bfloat16)],
        "expert_sum",
        12 * rows * width * hidden_units,
        10,
    )[0]


def own_sum(halves, hidden, back, other_back, shared, *earlier):
    numbers, named, router, weights = shared
    half, width = halves[0].shape
    hidden_units = weights[1].shape[0]
    return call(
        own_kernel,
        [numbers, *halves, named, router, *weights, *hidden, back, other_back, *earlier],
        [SMEM] + [VMEM] * 12 + [ANY] * len(earlier),
        [
            jax.ShapeDtypeStruct((half, width), jnp.bfloat16),
            jax.ShapeDtypeStruct((half, width), jnp.float32),
        ],
        [pltpu.VMEM((2, 2 * half, hidden_units), jnp.bfloat16)],
        "own_sum",
        24 * half * width * hidden_units,
        12,
    )


def after(values, *earlier):
    return pl.pallas_call(
        lambda *refs: None,
        in_specs=[ANY] * (len(values) + len(earlier)),
        out_specs=[ANY] * len(values),
        out_shape=[jax.ShapeDtypeStruct(x.shape, x.dtype) for x in values],
        input_output_aliases={number: number for number in range(len(values))},
        name="after",
        compiler_params=pltpu.CompilerParams(vmem_limit_bytes=MIB),
    )(*values, *earlier)


def chosen_kernel(outer, for_outer, for_inner, *refs):
    refs[-1][...] = jnp.where(outer[0:1, 0:1] > 0.0, for_outer[...], for_inner[...])


def added_kernel(one, other, *refs):
    total = one[...].astype(jnp.float32) + other[...].astype(jnp.float32)
    refs[-1][...] = total.astype(jnp.bfloat16)


def added_inside_kernel(outer, one, other, *refs):
    total = one[...].astype(jnp.float32) + other[...].astype(jnp.float32)
    refs[-1][...] = jnp.where(outer[0:1, 0:1] > 0.0, 0.0, total).astype(jnp.bfloat16)


def payload(kernel, inputs, earlier):
    one = inputs[-1]
    return call(
        kernel,
        [*inputs, *earlier],
        [VMEM] * len(inputs) + [ANY] * len(earlier),
        [jax.ShapeDtypeStruct(one.shape, one.dtype)],
        [],
        "payload",
        one.size,
        2,
    )[0]


def swap(values, axis, distance):
    size = lax.axis_size(axis)
    return lax.ppermute(values, axis, [(i, i ^ distance) for i in range(size)])


def gather_line(values):
    chips = lax.axis_size("exp") // 2
    return [values] + [swap(values, "exp", 2 * distance) for distance in range(1, chips)]


def gather_plane(line):
    return [swap(line, "req", distance) for distance in range(1, lax.axis_size("req"))]


def next_chip(values):
    size = lax.axis_size("exp")
    return lax.ppermute(values, "exp", [(i, (i + 2) % size) for i in range(size)])


def ring_experts(halves, hidden, shared, outer_here):
    chips = lax.axis_size("exp") // 2
    own = jnp.concatenate(halves, axis=0)
    rows, partial = own, None
    for step in range(1, chips):
        rows = next_chip(rows)
        plan = lambda chip, step=step: (True, lax.rem(chip + (chips - step), chips), 0)
        part = expert_sum(rows, rows, plan, shared, jnp.float32)
        if partial is not None:
            part = part + next_chip(partial).astype(jnp.float32)
        partial = part.astype(jnp.bfloat16)
    total = expert_sum(own, own, lambda chip: (True, chip, 0), shared, jnp.float32)
    if partial is not None:
        total = total + next_chip(partial).astype(jnp.float32)
    total = total + jnp.concatenate(hidden, axis=0).astype(jnp.float32)
    return total.astype(jnp.bfloat16)


COMPUTED = {
    2: ((1, 2, 1, 2), (0, 0, 0, 0)),
    3: ((2, 3, 0, 1), (0, 0, 0, 0)),
    4: ((3, 3, 0, 0), (0, 1, 1, 0)),
    5: ((3, 2, 1, 0), (1, 1, 1, 1)),
    6: ((2, 0, 3, 1), (1, 0, 0, 1)),
    7: ((1, 0, 3, 2), (1, 1, 1, 1)),
}


def by_chip(chip, numbers):
    found = numbers[0]
    for other, number in enumerate(numbers[1:], 1):
        found = jnp.where(chip == other, number, found)
    return found


def line_experts(halves, hidden, shared, outer_here):
    size = lax.axis_size("exp")
    first, second = halves
    half = first.shape[0]
    middle_pairs = [(i, i ^ (6 if 2 <= i < size - 2 else 1)) for i in range(size)]

    def chosen(for_outer, for_inner, *earlier):
        return payload(chosen_kernel, [outer_here, for_outer, for_inner], earlier)

    def added(one, other, *earlier):
        return payload(added_kernel, [one, other], earlier)

    side, middle, sums = {}, {}, {}

    def send_side(slot, *earlier):
        if slot == 2:
            rows = chosen(second, middle[1], *earlier)
        elif slot <= 5:
            rows = chosen(sums[slot - 1], middle[slot - 1], *earlier)
        elif slot == 6:
            rows = chosen(sums[5], second, middle[5], *earlier)
        else:
            rows = added(middle[slot - 1], sums[slot - 1], *earlier)
        side[slot] = swap(rows, "exp", 2)
        return rows

    def send_middle(slot, *earlier):
        if slot <= 3:
            rows = chosen(side[slot - 1], side[slot - 1], *earlier)
        elif slot == 4:
            rows = chosen(side[3], second, *earlier)
        else:
            inputs = [outer_here, side[slot - 1], sums[slot - 3]]
            rows = payload(added_inside_kernel, inputs, earlier)
        middle[slot] = lax.ppermute(rows, "exp", middle_pairs)
        return rows

    side[1] = swap(first, "exp", 2)
    middle[1] = lax.ppermute(first, "exp", middle_pairs)
    last = second
    for slot in range(2, 9):
        if slot % 2:
            sent = send_middle(slot, send_side(slot, last))
        else:
            sent = send_side(slot, send_middle(slot, last))
        if slot in COMPUTED:
            inner_rows = middle[slot - 1] if slot <= 5 else side[slot - 5]

            def plan(chip, slot=slot):
                owners, whichs = COMPUTED[slot]
                use_near = (chip == 0) | (chip == 3)
                start = pl.multiple_of(by_chip(chip, whichs) * half, half)
                return use_near, by_chip(chip, owners), start

            sums[slot] = expert_sum(side[slot - 1], inner_rows, plan, shared, jnp.bfloat16)
            last = sums[slot]
    back = chosen(side[7], side[3])
    upper, lower = own_sum(halves, hidden, back, middle[5], shared, sent)
    lower = lower + side[8].astype(jnp.float32) + middle[8].astype(jnp.float32)
    return jnp.concatenate([upper, lower.astype(jnp.bfloat16)], axis=0)


def on_device(
    tokens,
    token_request_slot,
    request_prompt,
    request_adapter,
    prompt_page_table,
    shared_prompt_cache,
    routes,
    attention_norm_gain,
    query_matrix,
    key_value_weight,
    attention_output_weight,
    adapter_query_down,
    adapter_query_up,
    adapter_output_down,
    adapter_output_up,
    expert_norm_gain,
    router,
    expert_gate_up,
    expert_down,
):
    count, width = tokens.shape
    requests = request_prompt.shape[0]
    experts = router.shape[1]
    other_gate_up = swap(expert_gate_up, "exp", 1)
    other_down = swap(expert_down, "exp", 1)
    page = shared_prompt_cache.shape[1:]
    pages_each = shared_prompt_cache.shape[0]
    where = jnp.stack([lax.axis_index("exp"), lax.axis_index("req")]).astype(jnp.int32)
    sizes = (lax.axis_size("exp"), lax.axis_size("req"))
    numbers, outer_here = call(
        functools.partial(prepare_kernel, pages_each, sizes),
        [where, token_request_slot, request_prompt, request_adapter, prompt_page_table],
        [SMEM, VMEM, SMEM, SMEM, SMEM],
        [
            jax.ShapeDtypeStruct((1 + 2 * requests + requests * PPP,), jnp.int32),
            jax.ShapeDtypeStruct((8, HEAD_WIDTH), jnp.float32),
        ],
        [],
        "prepare",
        count * width,
        4,
        [SMEM, VMEM],
    )
    route_rows = routes.T.reshape(-1, page[1]).astype(jnp.bfloat16)
    route_page = jnp.pad(route_rows, ((0, page[0] - route_rows.shape[0]), (0, 0)))
    blocks = gather_line(jnp.concatenate([shared_prompt_cache, route_page[None]], axis=0))
    line = jnp.concatenate([block[:pages_each] for block in blocks], axis=0)
    (line,) = after([line], outer_here)
    key_width = KEY_VALUE_HEADS * HEAD_WIDTH
    heads_width = query_matrix.shape[1]
    rank = adapter_query_down.shape[1]
    bfloat = lambda *shape: pltpu.VMEM(shape, jnp.bfloat16)
    query_rows, keys, values, named = call(
        functools.partial(projection_kernel, requests, routes.shape[1]),
        [
            numbers,
            attention_norm_gain,
            tokens,
            query_matrix,
            key_value_weight,
            adapter_query_down,
            adapter_query_up,
            *blocks,
        ],
        [SMEM, VMEM] + [ANY] * 5 + [VMEM] * len(blocks),
        [
            jax.ShapeDtypeStruct((count, columns), jnp.bfloat16)
            for columns in (heads_width, key_width, key_width)
        ]
        + [jax.ShapeDtypeStruct((len(blocks), count, experts), jnp.float32)],
        [
            bfloat(count, width),
            bfloat(heads_width // 512, width, 512),
            bfloat(width, 2 * key_width),
            bfloat(width, rank),
            bfloat(rank, heads_width),
            pltpu.SemaphoreType.DMA((4 + heads_width // 512,)),
        ],
        "projections",
        2 * count * width * (heads_width + 3 * key_width),
        52,
    )
    parts = after([line, *gather_plane(line)], keys)
    parts = [*parts] + [swap(part, "exp", 1) for part in parts]
    pages = len(parts) * parts[0].shape[0]
    half = count // 2
    rows_out = [jax.ShapeDtypeStruct((half, width), jnp.bfloat16)] * 2
    projected = [numbers, expert_norm_gain, query_rows, keys, values, tokens]
    output_weights = [attention_output_weight, adapter_output_down, adapter_output_up]
    weights = [expert_gate_up[0], expert_down[0], other_gate_up[0], other_down[0]]
    working = [
        bfloat(half, heads_width),
        pltpu.VMEM((half, width), jnp.float32),
        bfloat(half, width),
    ]
    hidden_first, first, prompt_rows, *held = call(
        functools.partial(fetch_kernel, requests, sizes[1], half),
        [*projected, *output_weights, *weights, *parts],
        [SMEM] + [VMEM] * 4 + [ANY] * (8 + len(parts)),
        rows_out
        + [bfloat(requests * PPP, *page)]
        + [bfloat(*weight.shape) for weight in output_weights + weights],
        [bfloat(pages, *page)]
        + working
        + [pltpu.SemaphoreType.DMA((number,)) for number in (len(parts), 7, 1)],
        "first_attention",
        2 * count * width * width,
        22,
    )
    hidden_second, second = call(
        functools.partial(attention_kernel, requests, half),
        [*projected, prompt_rows, *held[:3]],
        [SMEM] + [VMEM] * 4 + [ANY] + [VMEM] * 4,
        rows_out,
        working + [pltpu.SemaphoreType.DMA((1,))],
        "second_attention",
        2 * count * width * width,
        8,
    )
    shared = (numbers, named, router.T, held[3:])
    experts_of = line_experts if lax.axis_size("exp") == 8 else ring_experts
    return experts_of((first, second), (hidden_first, hidden_second), shared, outer_here)


def solution(mesh):
    return jax.shard_map(
        on_device,
        mesh=mesh,
        in_specs=(
            P(("req", "exp"), None),
            P(("req", "exp"), None),
            P(("req", "exp")),
            P(("req", "exp")),
            P(),
            P(("req", "exp"), None, None),
            P(("req", "exp"), None),
            P(),
            P(),
            P(),
            P(),
            P(),
            P(),
            P(),
            P(),
            P(),
            P(),
            P("exp", None, None),
            P("exp", None, None),
        ),
        out_specs=P(("req", "exp"), None),
        check_vma=False,
    )
```
